512 devices in a mesh: seg: 32 (over x, y), bond: 16 (over z, core).
Axes of the slice: x: 4, y: 8, z: 8, core: 2. Of those that a mesh axis runs over, the one named last changes fastest.
Arguments:
- env_in: bfloat16 [32, 16, 512, 512], P('seg', 'bond'), may hold values from -6 to 6
- site: bfloat16 [32, 16, 2, 512, 512], P('seg', 'bond'), may hold values from -0.125 to 0.125
- right_env: bfloat16 [32, 16, 512, 512], P('seg', 'bond'), may hold values from -18 to 18
- comp_ids: int32 [32, 4], P('seg'), may hold values from 0 to 2
- counts: int32 [32], P('seg'), may hold values from 1 to 4, as said below
Outputs:
- env_out: float32 [32, 16, 512, 512], P('seg', 'bond')
- corr: float32 [32], P('seg')
The draws below stay inside these ranges and needn't reach their ends.
Inputs may be any that keep to these rules, and one draw needn't show every extreme that they name: `counts`: some segment's list has length 4 in every draw.
All inputs are finite; a program needn't handle non-finite values.
Results may differ from the reference program's by a relative error of at most 0.00055.
Values may be sent and summed in bfloat16 or wider, within the bound.
A program may use at most 64 MiB of HBM per device.

```python
import jax
import jax.numpy as jnp
from jax import lax

CHI = 2048
PHYS = 2
KMAX = 4
SEGS = 32
GRID = 4
TILE = 512
N_BOND = 16


def draw_right_env(key, part):
    key = jax.random.fold_in(key, 11)
    rising = 3.0 ** (jnp.arange(N_BOND, dtype=jnp.float32) / max(N_BOND - 1, 1))
    values = jnp.clip(jax.random.normal(key, (SEGS, N_BOND, TILE, TILE), jnp.float32), -6.0, 6.0)
    return (values * rising[None, :, None, None]).astype(jnp.bfloat16)


def draw_counts(key, part):
    key = jax.random.fold_in(key, 5)
    first_key, second_key = jax.random.split(key)
    drawn = jax.random.randint(first_key, (SEGS,), 1, KMAX + 1, dtype=jnp.int32)
    full_spot = jax.random.randint(second_key, (), 0, SEGS, dtype=jnp.int32)
    return jnp.where(jnp.arange(SEGS, dtype=jnp.int32) == full_spot, KMAX, drawn).astype(jnp.int32)


def set_ends(result, key, least, largest):
    dims = result.shape
    index_at = [jax.random.randint(jax.random.fold_in(key, axis), (), 0, dims[axis]) for axis in range(len(dims))]
    result = result.at[tuple(index_at)].set(least)
    longest = dims.index(max(dims))
    index_at[longest] = (index_at[longest] + 1) % dims[longest]
    return result.at[tuple(index_at)].set(largest)


def steps_of(key, dims, shards, smallest, top_value):
    def one(axis_at, parts):
        heights = jax.random.uniform(jax.random.fold_in(jax.random.fold_in(key, 6), axis_at), (parts,), jnp.float32, smallest / len(shards), top_value / len(shards))
        return jnp.repeat(jnp.exp(heights), dims[axis_at] // parts).reshape((-1,) + (1,) * (len(dims) - axis_at - 1))

    gain = one(*shards[0])
    for cut in shards[1:]:
        gain = gain * one(*cut)
    return gain


def gaussian(own_key, extent, spread, limit, cuts=(), held_as=jnp.bfloat16):
    values = jax.random.normal(own_key, extent, jnp.float32) * spread
    if len(cuts) > 0:
        values = steps_of(own_key, extent, cuts, -0.22, 0.18) * values
    return jnp.clip(values, min=-limit, max=limit).astype(held_as)


def setup_inputs(seed: int = 0) -> dict:
    key_list = jax.random.split(jax.random.key(seed), 6)
    env_in = gaussian(key_list[0], (SEGS, N_BOND, TILE, TILE), 1.0, 6.0, ((0, 32), (1, 16)))
    site = gaussian(key_list[1], (SEGS, N_BOND, PHYS, TILE, TILE), CHI ** -0.5, 0.125, ((0, 32), (1, 16)))
    right_env = draw_right_env(jax.random.fold_in(key_list[5], 71), 0)
    comp_ids = set_ends(jax.random.randint(key_list[3], (SEGS, KMAX), 0, 3), jax.random.fold_in(key_list[3], 1), 0, 2).astype(jnp.int32)
    counts = draw_counts(jax.random.fold_in(key_list[5], 71), 0)
    return {"env_in": env_in, "site": site, "right_env": right_env, "comp_ids": comp_ids, "counts": counts}


def spin_table():
    return jnp.array([[[0.5, 0.0], [0.0, -0.5]], [[0.0, 0.5], [0.5, 0.0]], [[0.0, 0.5], [-0.5, 0.0]]], jnp.float32)


def local_operator(ids_row, count_now):
    active = jnp.arange(ids_row.shape[0], dtype=jnp.int32) < count_now
    matches = (ids_row[:, None] == jnp.arange(3, dtype=jnp.int32)[None, :]).astype(jnp.float32)
    tallies = jnp.sum(jnp.where(active[:, None], matches, jnp.zeros_like(matches)), axis=0)
    return jnp.einsum('c,cst->st', tallies, spin_table())


def to_matrix(blocks):
    return blocks.reshape(GRID, GRID, TILE, TILE).transpose(0, 2, 1, 3).reshape(CHI, CHI)


def to_blocks(matrix):
    return matrix.reshape(GRID, TILE, GRID, TILE).transpose(0, 2, 1, 3).reshape(N_BOND, TILE, TILE)


def push_segment(inputs):
    env_blocks, site_blocks, ids_row, count_now = inputs
    environment = to_matrix(env_blocks)
    site_up = to_matrix(site_blocks[:, 0])
    site_down = to_matrix(site_blocks[:, 1])
    operator = local_operator(ids_row, count_now)
    product_up = jnp.dot(environment, site_up, preferred_element_type=jnp.float32)
    product_down = jnp.dot(environment, site_down, preferred_element_type=jnp.float32)
    weighted_up = operator[0, 0] * product_up + operator[0, 1] * product_down
    weighted_down = operator[1, 0] * product_up + operator[1, 1] * product_down
    highest = lax.Precision.HIGHEST
    pushed = jnp.dot(site_up.T.astype(jnp.float32), weighted_up, precision=highest)
    pushed = pushed + jnp.dot(site_down.T.astype(jnp.float32), weighted_down, precision=highest)
    return to_blocks(pushed)


def reference(env_in, site, right_env, comp_ids, counts):
    env_out = lax.map(push_segment, (env_in, site, comp_ids, counts))
    arrived = jnp.concatenate([jnp.zeros((1, N_BOND, TILE, TILE), jnp.float32), env_out[:-1]], axis=0)
    corr = jnp.sum(arrived * right_env.astype(jnp.float32), axis=(1, 2, 3)) / CHI
    return env_out, corr
```

```python
import functools
import math

import jax
import jax.numpy as jnp
from jax import lax
from jax.experimental import pallas as pl
from jax.experimental.pallas import tpu as pltpu
from jax.sharding import PartitionSpec as P

MESH = pl.DeviceIdType.MESH
F32 = jnp.float32
BF16 = jnp.bfloat16


def kernel(
    side, bonds, segs,
    ids, counts, env, site, right,
    out, corr,
    e_all, a_all, w_acc, out_acc, right_in, term, terms_in,
    ring_send, ring_recv, e_send, e_recv, a_send, a_recv,
    right_send, right_recv, term_send, term_recv, local_sem,
):
    chips = bonds // 2
    seg = lax.axis_index("seg")
    bond = lax.axis_index("bond")
    z = bond // 2
    core = bond % 2
    row = bond // side
    column = bond % side
    half = z % 2
    turn = 1 - 2 * core

    def chip_at(step):
        return (z - turn * step + 2 * chips) % chips

    def mirrored(step):
        return (z + turn * step + 2 * chips) % chips

    def steps_from(chip, own_core):
        towards = jnp.where(own_core, z - chip, chip - z)
        return (towards * turn + 2 * chips) % chips

    following = (seg, ((z + turn + chips) % chips) * 2 + core)
    previous = (seg, ((z - turn + chips) % chips) * 2 + core)
    sibling = (seg, z * 2 + 1 - core)
    has_before = seg > 0
    has_after = seg < segs - 1

    barrier = pltpu.get_barrier_semaphore()
    pl.semaphore_signal(barrier, inc=1, device_id=previous, device_id_type=MESH)
    pl.semaphore_signal(barrier, inc=1, device_id=sibling, device_id_type=MESH)

    @pl.when(has_after)
    def _():
        pl.semaphore_signal(barrier, inc=1, device_id=(seg + 1, bond), device_id_type=MESH)

    @pl.when(has_before)
    def _():
        for peer in range(bonds):
            pl.semaphore_signal(barrier, inc=1, device_id=(seg - 1, peer), device_id_type=MESH)

    own_env = pltpu.make_async_copy(env.at[0, 0], e_all.at[bond], local_sem.at[0])
    own_site = pltpu.make_async_copy(site.at[0, 0], a_all.at[z], local_sem.at[1])
    own_env.start()
    own_site.start()
    w_acc[...] = jnp.zeros_like(w_acc)
    out_acc[...] = jnp.zeros_like(out_acc)

    pl.semaphore_wait(barrier, 2 + jnp.where(has_before, 1, 0) + jnp.where(has_after, bonds, 0))

    def ring_copy(step, part):
        chip = chip_at(step)
        if part == 0:
            ref = e_all.at[chip * 2 + core]
        else:
            ref = a_all.at[chip, part - 1]
        return pltpu.make_async_remote_copy(
            src_ref=ref, dst_ref=ref,
            send_sem=ring_send.at[step * 3 + part], recv_sem=ring_recv.at[step * 3 + part],
            device_id=following, device_id_type=MESH,
        )

    def ring_arrival(step, part):
        chip = chip_at(step)
        if part == 0:
            ref = e_all.at[chip * 2 + core]
        else:
            ref = a_all.at[chip, part - 1]
        return pltpu.make_async_remote_copy(
            src_ref=ref, dst_ref=ref,
            send_sem=ring_send.at[(step - 1) * 3 + part], recv_sem=ring_recv.at[(step - 1) * 3 + part],
            device_id=following, device_id_type=MESH,
        )

    def env_across(step, chip, at_core):
        ref = e_all.at[chip * 2 + at_core]
        return pltpu.make_async_remote_copy(
            src_ref=ref, dst_ref=ref, send_sem=e_send.at[step], recv_sem=e_recv.at[step],
            device_id=sibling, device_id_type=MESH,
        )

    def site_across(chip):
        return pltpu.make_async_remote_copy(
            src_ref=a_all.at[chip], dst_ref=a_all.at[chips + chip // 2],
            send_sem=a_send.at[chip // 2], recv_sem=a_recv.at[chip // 2],
            device_id=sibling, device_id_type=MESH,
        )

    def column_of(chip, at_core):
        return 2 * (chip % 2) + at_core

    def site_goes_on(step):
        target = (z + turn + chips) % chips
        return (step < chips - 2) | ((step == chips - 2) & (target // 2 == column_of(chip_at(step), core)))

    def site_comes(step):
        return (step < chips - 1) | ((step == chips - 1) & (row == column_of(chip_at(step), core)))

    own_env.wait()
    ring_copy(0, 0).start()
    own_site.wait()
    ring_copy(0, 1).start()
    ring_copy(0, 2).start()
    env_across(0, z, core).start()

    @pl.when(column_of(z, core) == row)
    def _():
        site_across(z).start()

    @pl.when(has_before)
    def _():
        pltpu.make_async_remote_copy(
            src_ref=right.at[0, 0], dst_ref=right_in, send_sem=right_send, recv_sem=right_recv,
            device_id=(seg - 1, bond), device_id_type=MESH,
        ).start()

    tally = [jnp.float32(0.0)] * 3
    for k in range(ids.shape[1]):
        for c in range(3):
            tally[c] = tally[c] + jnp.where((k < counts[0]) & (ids[0, k] == c), jnp.float32(1.0), jnp.float32(0.0))
    half_z = 0.5 * tally[0]
    operator = ((half_z, 0.5 * tally[1] + 0.5 * tally[2]), (0.5 * tally[1] - 0.5 * tally[2], -half_z))

    def env_step(a, k):
        return steps_from(2 * a + k // 2, k % 2 == core)

    def site_step(k):
        return steps_from(2 * k + half, jnp.bool_(True))

    def left_step(a):
        return steps_from(2 * a + row // 2, row % 2 == core)

    def compute(step):
        def first(i, carry):
            a = i // side
            k = i % side

            @pl.when(jnp.maximum(env_step(a, k), site_step(k)) == step)
            def _():
                block = e_all[a * side + k]
                for t in range(2):
                    w_acc[a, t] += jnp.dot(block, a_all[2 * k + half, t], preferred_element_type=F32)

            return carry

        lax.fori_loop(0, side * side, first, 0)

        def second(a, carry):
            latest = left_step(a)
            for k in range(side):
                latest = jnp.maximum(latest, jnp.maximum(env_step(a, k), site_step(k)))

            @pl.when(latest == step)
            def _():
                slot = jnp.where(row % 2 == core, 2 * a + row // 2, chips + a)
                for s in range(2):
                    weighted = operator[s][0] * w_acc[a, 0] + operator[s][1] * w_acc[a, 1]
                    high = weighted.astype(BF16)
                    low = (weighted - high.astype(F32)).astype(BF16)
                    left = a_all[slot, s]
                    dims = (((0,), (0,)), ((), ()))
                    out_acc[...] += lax.dot_general(left, high, dims, preferred_element_type=F32)
                    out_acc[...] += lax.dot_general(left, low, dims, preferred_element_type=F32)

            return carry

        lax.fori_loop(0, side, second, 0)

    def across_arrivals(step):
        chip = mirrored(step)
        env_across(step, chip, 1 - core).wait_recv()

        @pl.when((row % 2 != core) & (column_of(chip, 1 - core) == row))
        def _():
            site_across(chip).wait_recv()

    across_arrivals(0)
    compute(0)

    def turn_of(step, carry):
        ring_arrival(step, 0).wait_recv()

        @pl.when(step < chips - 1)
        def _():
            ring_copy(step, 0).start()

        env_across(step, chip_at(step), core).start()

        @pl.when(site_comes(step))
        def _():
            for part in (1, 2):
                ring_arrival(step, part).wait_recv()

                @pl.when(site_goes_on(step))
                def _():
                    ring_copy(step, part).start()

            @pl.when(column_of(chip_at(step), core) == row)
            def _():
                site_across(chip_at(step)).start()

        across_arrivals(step)
        compute(step)
        return carry

    lax.fori_loop(1, chips, turn_of, 0)

    store = pltpu.make_async_copy(out_acc, out.at[0, 0], local_sem.at[2])
    store.start()

    @pl.when(has_after)
    def _():
        pltpu.make_async_remote_copy(
            src_ref=right.at[0, 0], dst_ref=right_in, send_sem=right_send, recv_sem=right_recv,
            device_id=(seg, bond), device_id_type=MESH,
        ).wait_recv()
        size = out_acc.shape[0]
        products = out_acc[...] * right_in[...].astype(F32)
        folded = jnp.sum(products.reshape(size // 8, 8, size), axis=0)
        total = folded[:, :128]
        for at in range(128, size, 128):
            total = total + folded[:, at : at + 128]
        term[...] = total
        for peer in range(bonds):
            pltpu.make_async_remote_copy(
                src_ref=term, dst_ref=terms_in.at[bond], send_sem=term_send.at[peer], recv_sem=term_recv,
                device_id=(seg + 1, peer), device_id_type=MESH,
            ).start()

    corr[0] = jnp.float32(0.0)

    @pl.when(has_before)
    def _():
        pltpu.make_async_remote_copy(
            src_ref=terms_in, dst_ref=terms_in, send_sem=term_send.at[0], recv_sem=term_recv,
            device_id=(seg, bond), device_id_type=MESH,
        ).wait_recv()
        size = out_acc.shape[0] * side
        corr[0] = jnp.sum(terms_in[...]) * (1.0 / size)
        pltpu.make_async_remote_copy(
            src_ref=right.at[0, 0], dst_ref=right_in, send_sem=right_send, recv_sem=right_recv,
            device_id=(seg, bond), device_id_type=MESH,
        ).wait_send()

    @pl.when(has_after)
    def _():
        for peer in range(bonds):
            pltpu.make_async_remote_copy(
                src_ref=term, dst_ref=terms_in.at[bond], send_sem=term_send.at[peer], recv_sem=term_recv,
                device_id=(seg, bond), device_id_type=MESH,
            ).wait_send()

    def drain(step, carry):
        @pl.when(step < chips - 1)
        def _():
            ring_copy(step, 0).wait_send()

            @pl.when(site_goes_on(step))
            def _():
                ring_copy(step, 1).wait_send()
                ring_copy(step, 2).wait_send()

        env_across(step, chip_at(step), core).wait_send()

        @pl.when(column_of(chip_at(step), core) == row)
        def _():
            site_across(chip_at(step)).wait_send()

        return carry

    lax.fori_loop(0, chips, drain, 0)
    store.wait()


def body(env_in, site, right_env, comp_ids, counts):
    bonds = lax.axis_size("bond")
    segs = lax.axis_size("seg")
    side = math.isqrt(bonds)
    chips = bonds // 2
    size = env_in.shape[-1]
    hbm = pl.BlockSpec(memory_space=pl.ANY)
    smem = pl.BlockSpec(memory_space=pltpu.SMEM)
    dma = pltpu.SemaphoreType.DMA
    return pl.pallas_call(
        functools.partial(kernel, side, bonds, segs),
        out_shape=(
            jax.ShapeDtypeStruct((1, 1, size, size), F32),
            jax.ShapeDtypeStruct((1,), F32),
        ),
        in_specs=[smem, smem, hbm, hbm, hbm],
        out_specs=(hbm, smem),
        scratch_shapes=[
            pltpu.VMEM((bonds, size, size), BF16),
            pltpu.VMEM((chips + side, 2, size, size), BF16),
            pltpu.VMEM((side, 2, size, size), F32),
            pltpu.VMEM((size, size), F32),
            pltpu.VMEM((size, size), BF16),
            pltpu.VMEM((8, 128), F32),
            pltpu.VMEM((bonds, 8, 128), F32),
            dma((3 * (chips - 1),)),
            dma((3 * (chips - 1),)),
            dma((chips,)),
            dma((chips,)),
            dma((side,)),
            dma((side,)),
            dma,
            dma,
            dma((bonds,)),
            dma,
            dma((3,)),
        ],
        compiler_params=pltpu.CompilerParams(
            collective_id=0, has_side_effects=True, vmem_limit_bytes=56 * 2**20
        ),
        cost_estimate=pl.CostEstimate(flops=26 * 10**9, bytes_accessed=6 * 2**20, transcendentals=0),
    )(comp_ids, counts, env_in, site, right_env)


def solution(mesh):
    placed = (
        P("seg", "bond", None, None),
        P("seg", "bond", None, None, None),
        P("seg", "bond", None, None),
        P("seg", None),
        P("seg"),
    )
    return jax.shard_map(
        body,
        mesh=mesh,
        in_specs=placed,
        out_specs=(P("seg", "bond", None, None), P("seg")),
        check_vma=False,
    )
```

```python
import functools
import math

import jax
import jax.numpy as jnp
from jax import lax
from jax.experimental import pallas as pl
from jax.experimental.pallas import tpu as pltpu
from jax.sharding import PartitionSpec as P

MESH = pl.DeviceIdType.MESH
F32 = jnp.float32
BF16 = jnp.bfloat16


def kernel(
    side, bonds, segs,
    ids, counts, env, site, right,
    out, corr,
    e_all, a_all, w_acc, out_acc, parts, right_in, term, terms_in,
    ring_send, ring_recv, e_send, e_recv, a_send, a_recv,
    right_send, right_recv, term_send, term_recv, local_sem, line_ready,
):
    chips = bonds // 2
    seg = lax.axis_index("seg")
    bond = lax.axis_index("bond")
    z = bond // 2
    core = bond % 2
    row = bond // side
    column = bond % side
    half = z % 2
    turn = 1 - 2 * core

    def chip_at(step):
        return (z - turn * step + 2 * chips) % chips

    def mirrored(step):
        return (z + turn * step + 2 * chips) % chips

    def turned(chip):
        return (chip == chips // 4) | (chip == chips - 1 - chips // 4)

    def crossed(chip):
        return jnp.where(turned(chip) & (chip != z), 1, 0)

    def steps_from(chip, own_core):
        towards = jnp.where(own_core, z - chip, chip - z)
        return (towards * turn + 2 * chips) % chips

    following = (seg, ((z + turn + chips) % chips) * 2 + core)
    backward = (z - turn + chips) % chips
    sibling = (seg, z * 2 + 1 - core)
    has_before = seg > 0
    has_after = seg < segs - 1

    barrier = pltpu.get_barrier_semaphore()
    for peer in range(2):
        pl.semaphore_signal(barrier, inc=1, device_id=(seg, backward * 2 + peer), device_id_type=MESH)
    pl.semaphore_signal(barrier, inc=1, device_id=sibling, device_id_type=MESH)

    @pl.when(has_after)
    def _():
        pl.semaphore_signal(barrier, inc=1, device_id=(seg + 1, bond), device_id_type=MESH)

    own_env = pltpu.make_async_copy(env.at[0, 0], e_all.at[bond], local_sem.at[0])
    own_site = pltpu.make_async_copy(site.at[0, 0], a_all.at[z], local_sem.at[1])
    own_env.start()
    own_site.start()
    pl.semaphore_wait(barrier, 3 + jnp.where(has_before, 1, 0))

    def site_following(step):
        other = jnp.where(turned(z), step, 1) == 0
        return (seg, jnp.where(other, backward * 2 + 1 - core, following[1]))

    def ring_copy(step, part):
        chip = chip_at(step)
        if part == 0:
            ref = e_all.at[chip * 2 + core]
        else:
            ref = a_all.at[chip, part - 1]
        return pltpu.make_async_remote_copy(
            src_ref=ref, dst_ref=ref,
            send_sem=ring_send.at[step * 3 + part], recv_sem=ring_recv.at[step * 3 + part],
            device_id=following if part == 0 else site_following(step), device_id_type=MESH,
        )

    def ring_arrival(step, part):
        chip = chip_at(step)
        if part == 0:
            ref = e_all.at[chip * 2 + core]
        else:
            ref = a_all.at[chip, part - 1]
        return pltpu.make_async_remote_copy(
            src_ref=ref, dst_ref=ref,
            send_sem=ring_send.at[(step - 1) * 3 + part], recv_sem=ring_recv.at[(step - 1) * 3 + part],
            device_id=following, device_id_type=MESH,
        )

    def env_across(step, chip, at_core):
        ref = e_all.at[chip * 2 + at_core]
        return pltpu.make_async_remote_copy(
            src_ref=ref, dst_ref=ref, send_sem=e_send.at[step], recv_sem=e_recv.at[step],
            device_id=sibling, device_id_type=MESH,
        )

    def site_across(chip, from_core):
        across_slot = jnp.where(column_of(chip, from_core) == row, chip // 2, side)
        return pltpu.make_async_remote_copy(
            src_ref=a_all.at[chip], dst_ref=a_all.at[chips + across_slot],
            send_sem=a_send.at[across_slot], recv_sem=a_recv.at[across_slot],
            device_id=sibling, device_id_type=MESH,
        )

    def column_of(chip, at_core):
        return 2 * (chip % 2) + (at_core + crossed(chip)) % 2

    def needed_across(chip, from_core):
        found = column_of(chip, from_core)
        return (found == row) | (found == 2 * half + 1 - from_core)

    own_env.wait()
    ring_copy(0, 0).start()
    own_site.wait()
    ring_copy(0, 1).start()
    ring_copy(0, 2).start()
    env_across(0, z, core).start()

    @pl.when(needed_across(z, core))
    def _():
        site_across(z, core).start()

    @pl.when(has_before)
    def _():
        pltpu.make_async_remote_copy(
            src_ref=right.at[0, 0], dst_ref=right_in, send_sem=right_send, recv_sem=right_recv,
            device_id=(seg - 1, bond), device_id_type=MESH,
        ).start()

    w_acc[...] = jnp.zeros_like(w_acc)
    out_acc[...] = jnp.zeros_like(out_acc)

    tally = [jnp.float32(0.0)] * 3
    for k in range(ids.shape[1]):
        for c in range(3):
            tally[c] = tally[c] + jnp.where((k < counts[0]) & (ids[0, k] == c), jnp.float32(1.0), jnp.float32(0.0))
    half_z = 0.5 * tally[0]
    operator = ((half_z, 0.5 * tally[1] + 0.5 * tally[2]), (0.5 * tally[1] - 0.5 * tally[2], -half_z))

    def taken_up(chip, at_core):
        mine = at_core == core
        return 2 * steps_from(chip, mine) + jnp.where(mine, 0, 1)

    def env_step(a, k):
        return taken_up(2 * a + k // 2, k % 2)

    def site_step(k):
        chip = 2 * k + half
        return taken_up(chip, (core + crossed(chip)) % 2)

    def site_slot(k):
        chip = 2 * k + half
        return jnp.where(crossed(chip) == 0, chip, chips + jnp.where(column == row, k, side))

    def left_step(a):
        chip = 2 * a + row // 2
        return taken_up(chip, (row + crossed(chip)) % 2)

    def left_slot(a):
        chip = 2 * a + row // 2
        return jnp.where((row + crossed(chip)) % 2 == core, chip, chips + a)

    def compute(phase):
        def first(i, carry):
            a = i // side
            k = i % side

            @pl.when(jnp.maximum(env_step(a, k), site_step(k)) == phase)
            def _():
                block = e_all[a * side + k]
                slot = site_slot(k)
                for t in range(2):
                    w_acc[a, t] += jnp.dot(block, a_all[slot, t], preferred_element_type=F32)

            return carry

        lax.fori_loop(0, side * side, first, 0)

        def second(a, carry):
            latest = left_step(a)
            for k in range(side):
                latest = jnp.maximum(latest, jnp.maximum(env_step(a, k), site_step(k)))

            @pl.when(latest == phase)
            def _():
                slot = left_slot(a)
                size = out_acc.shape[0]
                for s in range(2):
                    weighted = operator[s][0] * w_acc[a, 0] + operator[s][1] * w_acc[a, 1]
                    high = weighted.astype(BF16)
                    parts[:, :size] = high
                    parts[:, size:] = (weighted - high.astype(F32)).astype(BF16)
                    dims = (((0,), (0,)), ((), ()))
                    both = lax.dot_general(a_all[slot, s], parts[...], dims, preferred_element_type=F32)
                    out_acc[...] += both[:, :size] + both[:, size:]

            return carry

        lax.fori_loop(0, side, second, 0)

    def across_arrivals(step):
        chip = mirrored(step)
        env_across(step, chip, 1 - core).wait_recv()

        @pl.when((step < chips - 1) & needed_across(chip, 1 - core))
        def _():
            site_across(chip, 1 - core).wait_recv()

    compute(0)

    def turn_of(step, carry):
        across_arrivals(step - 1)

        @pl.when((step == chips // 2 + 1) & has_before)
        def _():
            pl.semaphore_signal(line_ready, inc=1, device_id=(seg - 1, bond), device_id_type=MESH)

        compute(2 * step - 1)
        ring_arrival(step, 0).wait_recv()

        @pl.when(step < chips - 1)
        def _():
            ring_copy(step, 0).start()

        env_across(step, chip_at(step), core).start()

        @pl.when(step < chips - 1)
        def _():
            for part in (1, 2):
                ring_arrival(step, part).wait_recv()

                @pl.when(step < chips - 2)
                def _():
                    ring_copy(step, part).start()

            @pl.when(needed_across(chip_at(step), core))
            def _():
                site_across(chip_at(step), core).start()

        compute(2 * step)
        return carry

    lax.fori_loop(1, chips, turn_of, 0)
    across_arrivals(chips - 1)
    compute(2 * chips - 1)

    store = pltpu.make_async_copy(out_acc, out.at[0, 0], local_sem.at[2])
    store.start()

    @pl.when(has_after)
    def _():
        pltpu.make_async_remote_copy(
            src_ref=right.at[0, 0], dst_ref=right_in, send_sem=right_send, recv_sem=right_recv,
            device_id=(seg, bond), device_id_type=MESH,
        ).wait_recv()
        size = out_acc.shape[0]
        products = out_acc[...] * right_in[...].astype(F32)
        folded = jnp.sum(products.reshape(size // 8, 8, size), axis=0)
        total = folded[:, :128]
        for at in range(128, size, 128):
            total = total + folded[:, at : at + 128]
        term[...] = total
        pl.semaphore_wait(line_ready, 1)
        for peer in range(bonds):
            pltpu.make_async_remote_copy(
                src_ref=term, dst_ref=terms_in.at[bond], send_sem=term_send.at[peer], recv_sem=term_recv,
                device_id=(seg + 1, peer), device_id_type=MESH,
            ).start()

    corr[0] = jnp.float32(0.0)

    @pl.when(has_before)
    def _():
        pltpu.make_async_remote_copy(
            src_ref=terms_in, dst_ref=terms_in, send_sem=term_send.at[0], recv_sem=term_recv,
            device_id=(seg, bond), device_id_type=MESH,
        ).wait_recv()
        size = out_acc.shape[0] * side
        corr[0] = jnp.sum(terms_in[...]) * (1.0 / size)
        pltpu.make_async_remote_copy(
            src_ref=right.at[0, 0], dst_ref=right_in, send_sem=right_send, recv_sem=right_recv,
            device_id=(seg, bond), device_id_type=MESH,
        ).wait_send()

    @pl.when(has_after)
    def _():
        for peer in range(bonds):
            pltpu.make_async_remote_copy(
                src_ref=term, dst_ref=terms_in.at[bond], send_sem=term_send.at[peer], recv_sem=term_recv,
                device_id=(seg, bond), device_id_type=MESH,
            ).wait_send()

    def drain(step, carry):
        @pl.when(step < chips - 1)
        def _():
            ring_copy(step, 0).wait_send()

        @pl.when(step < chips - 2)
        def _():
            ring_copy(step, 1).wait_send()
            ring_copy(step, 2).wait_send()

        env_across(step, chip_at(step), core).wait_send()

        @pl.when((step < chips - 1) & needed_across(chip_at(step), core))
        def _():
            site_across(chip_at(step), core).wait_send()

        return carry

    lax.fori_loop(0, chips, drain, 0)
    store.wait()


def body(env_in, site, right_env, comp_ids, counts):
    bonds = lax.axis_size("bond")
    segs = lax.axis_size("seg")
    side = math.isqrt(bonds)
    chips = bonds // 2
    size = env_in.shape[-1]
    hbm = pl.BlockSpec(memory_space=pl.ANY)
    smem = pl.BlockSpec(memory_space=pltpu.SMEM)
    dma = pltpu.SemaphoreType.DMA
    return pl.pallas_call(
        functools.partial(kernel, side, bonds, segs),
        out_shape=(
            jax.ShapeDtypeStruct((1, 1, size, size), F32),
            jax.ShapeDtypeStruct((1,), F32),
        ),
        in_specs=[smem, smem, hbm, hbm, hbm],
        out_specs=(hbm, smem),
        scratch_shapes=[
            pltpu.VMEM((bonds, size, size), BF16),
            pltpu.VMEM((chips + side + 1, 2, size, size), BF16),
            pltpu.VMEM((side, 2, size, size), F32),
            pltpu.VMEM((size, size), F32),
            pltpu.VMEM((size, 2 * size), BF16),
            pltpu.VMEM((size, size), BF16),
            pltpu.VMEM((8, 128), F32),
            pltpu.VMEM((bonds, 8, 128), F32),
            dma((3 * (chips - 1),)),
            dma((3 * (chips - 1),)),
            dma((chips,)),
            dma((chips,)),
            dma((side + 1,)),
            dma((side + 1,)),
            dma,
            dma,
            dma((bonds,)),
            dma,
            dma((3,)),
            pltpu.SemaphoreType.REGULAR,
        ],
        compiler_params=pltpu.CompilerParams(
            collective_id=0, has_side_effects=True, vmem_limit_bytes=56 * 2**20
        ),
        cost_estimate=pl.CostEstimate(flops=26 * 10**9, bytes_accessed=6 * 2**20, transcendentals=0),
    )(comp_ids, counts, env_in, site, right_env)


def solution(mesh):
    placed = (
        P("seg", "bond", None, None),
        P("seg", "bond", None, None, None),
        P("seg", "bond", None, None),
        P("seg", None),
        P("seg"),
    )
    return jax.shard_map(
        body,
        mesh=mesh,
        in_specs=placed,
        out_specs=(P("seg", "bond", None, None), P("seg")),
        check_vma=False,
    )
```

```python
import functools
import math

import jax
import jax.numpy as jnp
from jax import lax
from jax.experimental import pallas as pl
from jax.experimental.pallas import tpu as pltpu
from jax.sharding import PartitionSpec as P

MESH = pl.DeviceIdType.MESH
F32 = jnp.float32
BF16 = jnp.bfloat16


def kernel(
    side, bonds, segs,
    ids, counts, env, site, right,
    out, corr,
    e_all, a_all, w_acc, out_acc, parts, right_in, term, terms_in,
    ring_send, ring_recv, e_send, e_recv, a_send, a_recv,
    right_send, right_recv, term_send, term_recv, local_sem, line_ready,
):
    chips = bonds // 2
    size = out_acc.shape[0]
    rows = size // 2
    seg = lax.axis_index("seg")
    bond = lax.axis_index("bond")
    z = bond // 2
    core = bond % 2
    row = bond // side
    column = bond % side
    half = z % 2
    turn = 1 - 2 * core

    def chip_at(step):
        return (z - turn * step + 2 * chips) % chips

    def mirrored(step):
        return (z + turn * step + 2 * chips) % chips

    def turned(chip):
        return (chip == chips // 4) | (chip == chips - 1 - chips // 4)

    def crossed(chip):
        return jnp.where(turned(chip) & (chip != z), 1, 0)

    def steps_from(chip, own_core):
        towards = jnp.where(own_core, z - chip, chip - z)
        return (towards * turn + 2 * chips) % chips

    following = (seg, ((z + turn + chips) % chips) * 2 + core)
    backward = (z - turn + chips) % chips
    sibling = (seg, z * 2 + 1 - core)
    has_before = seg > 0
    has_after = seg < segs - 1

    barrier = pltpu.get_barrier_semaphore()
    for peer in range(2):
        pl.semaphore_signal(barrier, inc=1, device_id=(seg, backward * 2 + peer), device_id_type=MESH)
    pl.semaphore_signal(barrier, inc=1, device_id=sibling, device_id_type=MESH)

    @pl.when(has_after)
    def _():
        pl.semaphore_signal(barrier, inc=1, device_id=(seg + 1, bond), device_id_type=MESH)

    own_env = pltpu.make_async_copy(env.at[0, 0], e_all.at[bond], local_sem.at[0])
    own_site = pltpu.make_async_copy(site.at[0, 0], a_all.at[z], local_sem.at[1])
    own_env.start()
    own_site.start()
    pl.semaphore_wait(barrier, 3 + jnp.where(has_before, 1, 0))

    def site_following(step):
        other = jnp.where(turned(z), step, 1) == 0
        return (seg, jnp.where(other, backward * 2 + 1 - core, following[1]))

    def ring_ref(step, part):
        chip = chip_at(step)
        if isinstance(part, int) and part >= 2:
            return a_all.at[chip, part - 2]
        return e_all.at[chip * 2 + core, pl.ds(part * rows, rows)]

    def ring_copy(step, part):
        ref = ring_ref(step, part)
        site_part = isinstance(part, int) and part >= 2
        return pltpu.make_async_remote_copy(
            src_ref=ref, dst_ref=ref,
            send_sem=ring_send.at[step * 4 + part], recv_sem=ring_recv.at[step * 4 + part],
            device_id=site_following(step) if site_part else following, device_id_type=MESH,
        )

    def ring_arrival(step, part):
        ref = ring_ref(step, part)
        return pltpu.make_async_remote_copy(
            src_ref=ref, dst_ref=ref,
            send_sem=ring_send.at[step * 4 - 4 + part], recv_sem=ring_recv.at[step * 4 - 4 + part],
            device_id=following, device_id_type=MESH,
        )

    def env_across(step, part, chip, at_core):
        ref = e_all.at[chip * 2 + at_core, pl.ds(part * rows, rows)]
        return pltpu.make_async_remote_copy(
            src_ref=ref, dst_ref=ref, send_sem=e_send.at[step * 2 + part], recv_sem=e_recv.at[step * 2 + part],
            device_id=sibling, device_id_type=MESH,
        )

    def site_across(chip, from_core, state):
        across_slot = jnp.where(column_of(chip, from_core) == row, chip // 2, side)
        return pltpu.make_async_remote_copy(
            src_ref=a_all.at[chip, state], dst_ref=a_all.at[chips + across_slot, state],
            send_sem=a_send.at[2 * across_slot + state], recv_sem=a_recv.at[2 * across_slot + state],
            device_id=sibling, device_id_type=MESH,
        )

    def column_of(chip, at_core):
        return 2 * (chip % 2) + (at_core + crossed(chip)) % 2

    def needed_across(chip, from_core):
        found = column_of(chip, from_core)
        return (found == row) | (found == 2 * half + 1 - from_core)

    own_site.wait()
    ring_copy(0, 2).start()
    ring_copy(0, 3).start()
    own_env.wait()
    ring_copy(0, 0).start()
    ring_copy(0, 1).start()
    env_across(0, 0, z, core).start()
    env_across(0, 1, z, core).start()

    @pl.when(needed_across(z, core))
    def _():
        for state in range(2):
            site_across(z, core, state).start()

    @pl.when(has_before)
    def _():
        pltpu.make_async_remote_copy(
            src_ref=right.at[0, 0], dst_ref=right_in, send_sem=right_send, recv_sem=right_recv,
            device_id=(seg - 1, bond), device_id_type=MESH,
        ).start()

    w_acc[...] = jnp.zeros_like(w_acc)
    out_acc[...] = jnp.zeros_like(out_acc)

    tally = [jnp.float32(0.0)] * 3
    for k in range(ids.shape[1]):
        for c in range(3):
            tally[c] = tally[c] + jnp.where((k < counts[0]) & (ids[0, k] == c), jnp.float32(1.0), jnp.float32(0.0))
    half_z = 0.5 * tally[0]
    operator = ((half_z, 0.5 * tally[1] + 0.5 * tally[2]), (0.5 * tally[1] - 0.5 * tally[2], -half_z))

    def env_phase(a, k):
        mine = k % 2 == core
        return 6 * steps_from(2 * a + k // 2, mine) + jnp.where(mine, 2, 4)

    def site_phase(chip, at_core):
        mine = at_core == core
        return 6 * steps_from(chip, mine) + jnp.where(mine, 0, 1)

    def column_phase(k):
        chip = 2 * k + half
        return site_phase(chip, (core + crossed(chip)) % 2)

    def column_slot(k):
        chip = 2 * k + half
        return jnp.where(crossed(chip) == 0, chip, chips + jnp.where(column == row, k, side))

    def left_phase(a):
        chip = 2 * a + row // 2
        return site_phase(chip, (row + crossed(chip)) % 2)

    def left_slot(a):
        chip = 2 * a + row // 2
        return jnp.where((row + crossed(chip)) % 2 == core, chip, chips + a)

    all_columns = jnp.int32(0)
    for k in range(side):
        all_columns = jnp.maximum(all_columns, column_phase(k))
    last_env = []
    last_site = []
    for a in range(side):
        latest = env_phase(a, 0)
        for k in range(1, side):
            latest = jnp.maximum(latest, env_phase(a, k))
        last_env.append(latest)
        last_site.append(jnp.maximum(all_columns, left_phase(a)))

    def picked(values, a):
        found = values[side - 1]
        for at in range(side - 1):
            found = jnp.where(a == at, values[at], found)
        return found

    def add_product(a, k, part, states):
        block = e_all[a * side + k, pl.ds(part * rows, rows)]
        slot = column_slot(k)
        for t in states:
            w_acc[a, t, pl.ds(part * rows, rows)] += jnp.dot(block, a_all[slot, t], preferred_element_type=F32)

    def finish(a, part, phase):
        @pl.when(jnp.maximum(picked(last_env, a) + part, picked(last_site, a)) == phase)
        def _():
            here = pl.ds(part * rows, rows)
            for s in range(2):
                weighted = operator[s][0] * w_acc[a, 0, here] + operator[s][1] * w_acc[a, 1, here]
                high = weighted.astype(BF16)
                parts[s * rows : (s + 1) * rows, :size] = high
                parts[s * rows : (s + 1) * rows, size:] = (weighted - high.astype(F32)).astype(BF16)
            left = a_all[left_slot(a), :, here].reshape(size, size)
            both = lax.dot_general(left, parts[...], (((0,), (0,)), ((), ())), preferred_element_type=F32)
            out_acc[...] += both[:, :size] + both[:, size:]

    def take_env(chip, at_core, part, phase):
        a = chip // 2
        k = 2 * (chip % 2) + at_core

        @pl.when(column_phase(k) < phase)
        def _():
            add_product(a, k, part, (0, 1))

        finish(a, part, phase)

    def take_site(chip, at_core, phase, state):
        k = chip // 2

        def one(i, carry):
            a = i // 2
            part = i % 2

            @pl.when(env_phase(a, k) + part < phase)
            def _():
                add_product(a, k, part, (state,))

            return carry

        @pl.when(column_of(chip, at_core) == column)
        def _():
            lax.fori_loop(0, 2 * side, one, 0)

    def finish_site(chip, at_core, phase):
        found = column_of(chip, at_core)

        def one(i, carry):
            finish(i // 2, i % 2, phase)
            return carry

        @pl.when((found == column) | (found == row))
        def _():
            lax.fori_loop(0, 2 * side, one, 0)

    def own_halves(step):
        def one(part, carry):
            @pl.when(step > 0)
            def _():
                ring_arrival(step, part).wait_recv()

                @pl.when(step < chips - 1)
                def _():
                    ring_copy(step, part).start()

                env_across(step, part, chip_at(step), core).start()

            take_env(chip_at(step), core, part, 6 * step + 2 + part)
            return carry

        lax.fori_loop(0, 2, one, 0)

    def across_halves(step):
        chip = mirrored(step)

        def one(part, carry):
            env_across(step, part, chip, 1 - core).wait_recv()
            take_env(chip, 1 - core, part, 6 * step + 4 + part)
            return carry

        lax.fori_loop(0, 2, one, 0)

    def own_site(step):
        chip = chip_at(step)
        for state in range(2):
            @pl.when(step > 0)
            def _():
                ring_arrival(step, 2 + state).wait_recv()

                @pl.when(step < chips - 2)
                def _():
                    ring_copy(step, 2 + state).start()

                @pl.when(needed_across(chip, core))
                def _():
                    site_across(chip, core, state).start()

            take_site(chip, core, 6 * step, state)

    def sibling_site(step):
        chip = mirrored(step)

        @pl.when(needed_across(chip, 1 - core))
        def _():
            for state in range(2):
                site_across(chip, 1 - core, state).wait_recv()
                take_site(chip, 1 - core, 6 * step + 1, state)

    def turn_of(step, carry):
        @pl.when(step < chips - 1)
        def _():
            own_site(step)
            sibling_site(step)

        own_halves(step)

        @pl.when(step < chips - 1)
        def _():
            finish_site(chip_at(step), core, 6 * step)

            @pl.when(needed_across(mirrored(step), 1 - core))
            def _():
                finish_site(mirrored(step), 1 - core, 6 * step + 1)

        @pl.when((step == chips // 2 + 1) & has_before)
        def _():
            pl.semaphore_signal(line_ready, inc=1, device_id=(seg - 1, bond), device_id_type=MESH)

        across_halves(step)
        return carry

    lax.fori_loop(0, chips, turn_of, 0)

    store = pltpu.make_async_copy(out_acc, out.at[0, 0], local_sem.at[2])
    store.start()

    @pl.when(has_after)
    def _():
        pltpu.make_async_remote_copy(
            src_ref=right.at[0, 0], dst_ref=right_in, send_sem=right_send, recv_sem=right_recv,
            device_id=(seg, bond), device_id_type=MESH,
        ).wait_recv()
        products = out_acc[...] * right_in[...].astype(F32)
        folded = jnp.sum(products.reshape(size // 8, 8, size), axis=0)
        total = folded[:, :128]
        for at in range(128, size, 128):
            total = total + folded[:, at : at + 128]
        term[...] = total
        pl.semaphore_wait(line_ready, 1)
        for peer in range(bonds):
            pltpu.make_async_remote_copy(
                src_ref=term, dst_ref=terms_in.at[bond], send_sem=term_send.at[peer], recv_sem=term_recv,
                device_id=(seg + 1, peer), device_id_type=MESH,
            ).start()

    corr[0] = jnp.float32(0.0)

    @pl.when(has_before)
    def _():
        pltpu.make_async_remote_copy(
            src_ref=terms_in, dst_ref=terms_in, send_sem=term_send.at[0], recv_sem=term_recv,
            device_id=(seg, bond), device_id_type=MESH,
        ).wait_recv()
        corr[0] = jnp.sum(terms_in[...]) * (1.0 / (size * side))
        pltpu.make_async_remote_copy(
            src_ref=right.at[0, 0], dst_ref=right_in, send_sem=right_send, recv_sem=right_recv,
            device_id=(seg, bond), device_id_type=MESH,
        ).wait_send()

    @pl.when(has_after)
    def _():
        for peer in range(bonds):
            pltpu.make_async_remote_copy(
                src_ref=term, dst_ref=terms_in.at[bond], send_sem=term_send.at[peer], recv_sem=term_recv,
                device_id=(seg, bond), device_id_type=MESH,
            ).wait_send()

    def drain(step, carry):
        @pl.when(step < chips - 1)
        def _():
            ring_copy(step, 0).wait_send()
            ring_copy(step, 1).wait_send()

        @pl.when(step < chips - 2)
        def _():
            ring_copy(step, 2).wait_send()
            ring_copy(step, 3).wait_send()

        env_across(step, 0, chip_at(step), core).wait_send()
        env_across(step, 1, chip_at(step), core).wait_send()

        @pl.when((step < chips - 1) & needed_across(chip_at(step), core))
        def _():
            for state in range(2):
                site_across(chip_at(step), core, state).wait_send()

        return carry

    lax.fori_loop(0, chips, drain, 0)
    store.wait()


def body(env_in, site, right_env, comp_ids, counts):
    bonds = lax.axis_size("bond")
    segs = lax.axis_size("seg")
    side = math.isqrt(bonds)
    chips = bonds // 2
    size = env_in.shape[-1]
    hbm = pl.BlockSpec(memory_space=pl.ANY)
    smem = pl.BlockSpec(memory_space=pltpu.SMEM)
    dma = pltpu.SemaphoreType.DMA
    return pl.pallas_call(
        functools.partial(kernel, side, bonds, segs),
        out_shape=(
            jax.ShapeDtypeStruct((1, 1, size, size), F32),
            jax.ShapeDtypeStruct((1,), F32),
        ),
        in_specs=[smem, smem, hbm, hbm, hbm],
        out_specs=(hbm, smem),
        scratch_shapes=[
            pltpu.VMEM((bonds, size, size), BF16),
            pltpu.VMEM((chips + side + 1, 2, size, size), BF16),
            pltpu.VMEM((side, 2, size, size), F32),
            pltpu.VMEM((size, size), F32),
            pltpu.VMEM((size, 2 * size), BF16),
            pltpu.VMEM((size, size), BF16),
            pltpu.VMEM((8, 128), F32),
            pltpu.VMEM((bonds, 8, 128), F32),
            dma((4 * (chips - 1),)),
            dma((4 * (chips - 1),)),
            dma((2 * chips,)),
            dma((2 * chips,)),
            dma((2 * side + 2,)),
            dma((2 * side + 2,)),
            dma,
            dma,
            dma((bonds,)),
            dma,
            dma((3,)),
            pltpu.SemaphoreType.REGULAR,
        ],
        compiler_params=pltpu.CompilerParams(
            collective_id=0, has_side_effects=True, vmem_limit_bytes=56 * 2**20
        ),
        cost_estimate=pl.CostEstimate(flops=26 * 10**9, bytes_accessed=6 * 2**20, transcendentals=0),
    )(comp_ids, counts, env_in, site, right_env)


def solution(mesh):
    placed = (
        P("seg", "bond", None, None),
        P("seg", "bond", None, None, None),
        P("seg", "bond", None, None),
        P("seg", None),
        P("seg"),
    )
    return jax.shard_map(
        body,
        mesh=mesh,
        in_specs=placed,
        out_specs=(P("seg", "bond", None, None), P("seg")),
        check_vma=False,
    )
```

```python
import functools
import math

import jax
import jax.numpy as jnp
from jax import lax
from jax.experimental import pallas as pl
from jax.experimental.pallas import tpu as pltpu
from jax.sharding import PartitionSpec as P

MESH = pl.DeviceIdType.MESH
F32 = jnp.float32
BF16 = jnp.bfloat16


def kernel(
    side, bonds, segs,
    ids, counts, env, site, right,
    out, corr,
    e_all, a_all, w_acc, parts, right_in, term, terms_in,
    ring_send, ring_recv, e_send, e_recv, a_send, a_recv,
    right_send, right_recv, term_send, term_recv, local_sem, line_ready,
):
    chips = bonds // 2
    out_acc = out.at[0, 0]
    size = out_acc.shape[0]
    rows = size // 2
    seg = lax.axis_index("seg")
    bond = lax.axis_index("bond")
    z = bond // 2
    core = bond % 2
    row = bond // side
    column = bond % side
    half = z % 2
    turn = 1 - 2 * core

    def chip_at(step):
        return (z - turn * step + 2 * chips) % chips

    def mirrored(step):
        return (z + turn * step + 2 * chips) % chips

    def turned(chip):
        return (chip == chips // 4) | (chip == chips - 1 - chips // 4)

    def crossed(chip):
        return jnp.where(turned(chip) & (chip != z), 1, 0)

    def steps_from(chip, own_core):
        towards = jnp.where(own_core, z - chip, chip - z)
        return (towards * turn + 2 * chips) % chips

    following = (seg, ((z + turn + chips) % chips) * 2 + core)
    backward = (z - turn + chips) % chips
    sibling = (seg, z * 2 + 1 - core)
    has_before = seg > 0
    has_after = seg < segs - 1

    barrier = pltpu.get_barrier_semaphore()
    for peer in range(2):
        pl.semaphore_signal(barrier, inc=1, device_id=(seg, backward * 2 + peer), device_id_type=MESH)
    pl.semaphore_signal(barrier, inc=1, device_id=sibling, device_id_type=MESH)

    @pl.when(has_after)
    def _():
        pl.semaphore_signal(barrier, inc=1, device_id=(seg + 1, bond), device_id_type=MESH)

    own_env = pltpu.make_async_copy(env.at[0, 0], e_all.at[bond], local_sem.at[0])
    own_site = pltpu.make_async_copy(site.at[0, 0], a_all.at[z], local_sem.at[1])
    own_env.start()
    own_site.start()
    pl.semaphore_wait(barrier, 3 + jnp.where(has_before, 1, 0))

    def site_following(step):
        other = jnp.where(turned(z), step, 1) == 0
        return (seg, jnp.where(other, backward * 2 + 1 - core, following[1]))

    def ring_ref(step, part):
        chip = chip_at(step)
        if isinstance(part, int) and part >= 2:
            return a_all.at[chip, part - 2]
        return e_all.at[chip * 2 + core, pl.ds(part * rows, rows)]

    def ring_copy(step, part):
        ref = ring_ref(step, part)
        site_part = isinstance(part, int) and part >= 2
        return pltpu.make_async_remote_copy(
            src_ref=ref, dst_ref=ref,
            send_sem=ring_send.at[step * 4 + part], recv_sem=ring_recv.at[step * 4 + part],
            device_id=site_following(step) if site_part else following, device_id_type=MESH,
        )

    def ring_arrival(step, part):
        ref = ring_ref(step, part)
        return pltpu.make_async_remote_copy(
            src_ref=ref, dst_ref=ref,
            send_sem=ring_send.at[step * 4 - 4 + part], recv_sem=ring_recv.at[step * 4 - 4 + part],
            device_id=following, device_id_type=MESH,
        )

    def env_across(step, part, chip, at_core):
        ref = e_all.at[chip * 2 + at_core, pl.ds(part * rows, rows)]
        return pltpu.make_async_remote_copy(
            src_ref=ref, dst_ref=ref, send_sem=e_send.at[step * 2 + part], recv_sem=e_recv.at[step * 2 + part],
            device_id=sibling, device_id_type=MESH,
        )

    def site_across(chip, from_core, state):
        across_slot = jnp.where(column_of(chip, from_core) == row, chip // 2, side)
        return pltpu.make_async_remote_copy(
            src_ref=a_all.at[chip, state], dst_ref=a_all.at[chips + across_slot, state],
            send_sem=a_send.at[2 * across_slot + state], recv_sem=a_recv.at[2 * across_slot + state],
            device_id=sibling, device_id_type=MESH,
        )

    def column_of(chip, at_core):
        return 2 * (chip % 2) + (at_core + crossed(chip)) % 2

    def needed_across(chip, from_core):
        found = column_of(chip, from_core)
        return (found == row) | (found == 2 * half + 1 - from_core)

    own_site.wait()
    ring_copy(0, 2).start()
    ring_copy(0, 3).start()
    own_env.wait()
    ring_copy(0, 0).start()
    ring_copy(0, 1).start()
    env_across(0, 0, z, core).start()
    env_across(0, 1, z, core).start()

    @pl.when(needed_across(z, core))
    def _():
        for state in range(2):
            site_across(z, core, state).start()

    @pl.when(has_before)
    def _():
        pltpu.make_async_remote_copy(
            src_ref=right.at[0, 0], dst_ref=right_in, send_sem=right_send, recv_sem=right_recv,
            device_id=(seg - 1, bond), device_id_type=MESH,
        ).start()

    w_acc[...] = jnp.zeros_like(w_acc)
    out_acc[...] = jnp.zeros_like(out_acc)

    tally = [jnp.float32(0.0)] * 3
    for k in range(ids.shape[1]):
        for c in range(3):
            tally[c] = tally[c] + jnp.where((k < counts[0]) & (ids[0, k] == c), jnp.float32(1.0), jnp.float32(0.0))
    doubled = ((tally[0], tally[1] + tally[2]), (tally[1] - tally[2], -tally[0]))

    def env_phase(a, k):
        mine = k % 2 == core
        return 6 * steps_from(2 * a + k // 2, mine) + jnp.where(mine, 2, 4)

    def site_phase(chip, at_core):
        mine = at_core == core
        return 6 * steps_from(chip, mine) + jnp.where(mine, 0, 1)

    def column_phase(k):
        chip = 2 * k + half
        return site_phase(chip, (core + crossed(chip)) % 2)

    def column_slot(k):
        chip = 2 * k + half
        return jnp.where(crossed(chip) == 0, chip, chips + jnp.where(column == row, k, side))

    def left_phase(a):
        chip = 2 * a + row // 2
        return site_phase(chip, (row + crossed(chip)) % 2)

    def left_slot(a):
        chip = 2 * a + row // 2
        return jnp.where((row + crossed(chip)) % 2 == core, chip, chips + a)

    all_columns = jnp.int32(0)
    for k in range(side):
        all_columns = jnp.maximum(all_columns, column_phase(k))
    last_env = []
    last_site = []
    for a in range(side):
        latest = env_phase(a, 0)
        for k in range(1, side):
            latest = jnp.maximum(latest, env_phase(a, k))
        last_env.append(latest)
        last_site.append(jnp.maximum(all_columns, left_phase(a)))

    def picked(values, a):
        found = values[side - 1]
        for at in range(side - 1):
            found = jnp.where(a == at, values[at], found)
        return found

    def add_product(a, k, part, states):
        block = e_all[a * side + k, pl.ds(part * rows, rows)]
        slot = column_slot(k)
        for t in states:
            w_acc[a, t, pl.ds(part * rows, rows)] += jnp.dot(block, a_all[slot, t], preferred_element_type=F32)

    def finish(a, part, phase):
        @pl.when(jnp.maximum(picked(last_env, a) + part, picked(last_site, a)) == phase)
        def _():
            here = pl.ds(part * rows, rows)
            for s in range(2):
                weighted = doubled[s][0] * w_acc[a, 0, here] + doubled[s][1] * w_acc[a, 1, here]
                high = weighted.astype(BF16)
                parts[s * rows : (s + 1) * rows, :size] = high
                parts[s * rows : (s + 1) * rows, size:] = (weighted - high.astype(F32)).astype(BF16)
            left = a_all[left_slot(a), :, here].reshape(size, size)
            both = lax.dot_general(left, parts[...], (((0,), (0,)), ((), ())), preferred_element_type=F32)
            out_acc[...] += both[:, :size] + both[:, size:]

    def take_env(chip, at_core, part, phase):
        a = chip // 2
        k = 2 * (chip % 2) + at_core

        @pl.when(column_phase(k) < phase)
        def _():
            add_product(a, k, part, (0, 1))

        finish(a, part, phase)

    def take_site(chip, at_core, phase, state):
        k = chip // 2

        def one(i, carry):
            a = i // 2
            part = i % 2

            @pl.when(env_phase(a, k) + part < phase)
            def _():
                add_product(a, k, part, (state,))

            return carry

        @pl.when(column_of(chip, at_core) == column)
        def _():
            lax.fori_loop(0, 2 * side, one, 0)

    def finish_site(chip, at_core, phase):
        found = column_of(chip, at_core)

        def one(i, carry):
            finish(i // 2, i % 2, phase)
            return carry

        @pl.when((found == column) | (found == row))
        def _():
            lax.fori_loop(0, 2 * side, one, 0)

    def env_comes(step, part):
        @pl.when(step > 0)
        def _():
            ring_arrival(step, part).wait_recv()
            ring_copy(step, part).start()
            env_across(step, part, chip_at(step), core).start()

    def own_halves(step):
        def one(part, carry):
            take_env(chip_at(step), core, part, 6 * step + 2 + part)
            return carry

        lax.fori_loop(0, 2, one, 0)

    def across_halves(step):
        chip = mirrored(step)

        def one(part, carry):
            env_across(step, part, chip, 1 - core).wait_recv()
            take_env(chip, 1 - core, part, 6 * step + 4 + part)
            return carry

        lax.fori_loop(0, 2, one, 0)

    def own_site(step, state):
        chip = chip_at(step)

        @pl.when(step > 0)
        def _():
            ring_arrival(step, 2 + state).wait_recv()

            @pl.when(step < chips - 2)
            def _():
                ring_copy(step, 2 + state).start()

            @pl.when(needed_across(chip, core))
            def _():
                site_across(chip, core, state).start()

        take_site(chip, core, 6 * step, state)

    def sibling_site(step, state):
        chip = mirrored(step)

        @pl.when(column_of(chip, 1 - core) == column)
        def _():
            site_across(chip, 1 - core, state).wait_recv()
            take_site(chip, 1 - core, 6 * step + 1, state)

    def turn_of(step, carry):
        own_site(step, 0)
        sibling_site(step, 0)
        own_site(step, 1)
        env_comes(step, 0)
        sibling_site(step, 1)
        env_comes(step, 1)
        own_halves(step)
        finish_site(chip_at(step), core, 6 * step)
        chip = mirrored(step)

        @pl.when(needed_across(chip, 1 - core))
        def _():
            @pl.when(column_of(chip, 1 - core) != column)
            def _():
                for state in range(2):
                    site_across(chip, 1 - core, state).wait_recv()

            finish_site(chip, 1 - core, 6 * step + 1)

        @pl.when((step == chips // 2 + 1) & has_before)
        def _():
            pl.semaphore_signal(line_ready, inc=1, device_id=(seg - 1, bond), device_id_type=MESH)

        across_halves(step)
        return carry

    lax.fori_loop(0, chips - 1, turn_of, 0)

    def last_turn(part, carry):
        step = chips - 1
        ring_arrival(step, part).wait_recv()
        env_across(step, part, chip_at(step), core).start()
        take_env(chip_at(step), core, part, 6 * step + 2 + part)
        env_across(step, part, mirrored(step), 1 - core).wait_recv()
        take_env(mirrored(step), 1 - core, part, 6 * step + 4 + part)
        return carry

    lax.fori_loop(0, 2, last_turn, 0)

    @pl.when(has_after)
    def _():
        pltpu.make_async_remote_copy(
            src_ref=right.at[0, 0], dst_ref=right_in, send_sem=right_send, recv_sem=right_recv,
            device_id=(seg, bond), device_id_type=MESH,
        ).wait_recv()
        products = out_acc[...] * right_in[...].astype(F32)
        folded = jnp.sum(products.reshape(size // 8, 8, size), axis=0)
        total = folded[:, :128]
        for at in range(128, size, 128):
            total = total + folded[:, at : at + 128]
        term[...] = total
        pl.semaphore_wait(line_ready, 1)
        for peer in range(bonds):
            pltpu.make_async_remote_copy(
                src_ref=term, dst_ref=terms_in.at[bond], send_sem=term_send.at[peer], recv_sem=term_recv,
                device_id=(seg + 1, peer), device_id_type=MESH,
            ).start()

    corr[0] = jnp.float32(0.0)

    @pl.when(has_before)
    def _():
        pltpu.make_async_remote_copy(
            src_ref=terms_in, dst_ref=terms_in, send_sem=term_send.at[0], recv_sem=term_recv,
            device_id=(seg, bond), device_id_type=MESH,
        ).wait_recv()
        corr[0] = jnp.sum(terms_in[...]) * (0.5 / (size * side))
        pltpu.make_async_remote_copy(
            src_ref=right.at[0, 0], dst_ref=right_in, send_sem=right_send, recv_sem=right_recv,
            device_id=(seg, bond), device_id_type=MESH,
        ).wait_send()

    @pl.when(has_after)
    def _():
        for peer in range(bonds):
            pltpu.make_async_remote_copy(
                src_ref=term, dst_ref=terms_in.at[bond], send_sem=term_send.at[peer], recv_sem=term_recv,
                device_id=(seg, bond), device_id_type=MESH,
            ).wait_send()

    def drain(step, carry):
        @pl.when(step < chips - 1)
        def _():
            ring_copy(step, 0).wait_send()
            ring_copy(step, 1).wait_send()

        @pl.when(step < chips - 2)
        def _():
            ring_copy(step, 2).wait_send()
            ring_copy(step, 3).wait_send()

        env_across(step, 0, chip_at(step), core).wait_send()
        env_across(step, 1, chip_at(step), core).wait_send()

        @pl.when((step < chips - 1) & needed_across(chip_at(step), core))
        def _():
            for state in range(2):
                site_across(chip_at(step), core, state).wait_send()

        return carry

    lax.fori_loop(0, chips, drain, 0)


def body(env_in, site, right_env, comp_ids, counts):
    bonds = lax.axis_size("bond")
    segs = lax.axis_size("seg")
    side = math.isqrt(bonds)
    chips = bonds // 2
    size = env_in.shape[-1]
    hbm = pl.BlockSpec(memory_space=pltpu.HBM)
    smem = pl.BlockSpec(memory_space=pltpu.SMEM)
    dma = pltpu.SemaphoreType.DMA
    twice, closed = pl.pallas_call(
        functools.partial(kernel, side, bonds, segs),
        out_shape=(
            pltpu.VMEM((1, 1, size, size), F32),
            jax.ShapeDtypeStruct((1,), F32),
        ),
        in_specs=[smem, smem, hbm, hbm, hbm],
        out_specs=(pl.BlockSpec(memory_space=pltpu.VMEM), smem),
        scratch_shapes=[
            pltpu.VMEM((bonds, size, size), BF16),
            pltpu.VMEM((chips + side + 1, 2, size, size), BF16),
            pltpu.VMEM((side, 2, size, size), F32),
            pltpu.VMEM((size, 2 * size), BF16),
            pltpu.VMEM((size, size), BF16),
            pltpu.VMEM((8, 128), F32),
            pltpu.VMEM((bonds, 8, 128), F32),
            dma((4 * (chips - 1),)),
            dma((4 * (chips - 1),)),
            dma((2 * chips,)),
            dma((2 * chips,)),
            dma((2 * side + 2,)),
            dma((2 * side + 2,)),
            dma,
            dma,
            dma((bonds,)),
            dma,
            dma((2,)),
            pltpu.SemaphoreType.REGULAR,
        ],
        compiler_params=pltpu.CompilerParams(
            collective_id=0, has_side_effects=True, vmem_limit_bytes=56 * 2**20
        ),
        cost_estimate=pl.CostEstimate(flops=26 * 10**9, bytes_accessed=6 * 2**20, transcendentals=0),
    )(comp_ids, counts, env_in, site, right_env)
    return twice * 0.5, closed


def solution(mesh):
    placed = (
        P("seg", "bond", None, None),
        P("seg", "bond", None, None, None),
        P("seg", "bond", None, None),
        P("seg", None),
        P("seg"),
    )
    return jax.shard_map(
        body,
        mesh=mesh,
        in_specs=placed,
        out_specs=(P("seg", "bond", None, None), P("seg")),
        check_vma=False,
    )
```

```python
import functools
import math

import jax
import jax.numpy as jnp
from jax import lax
from jax.experimental import pallas as pl
from jax.experimental.pallas import tpu as pltpu
from jax.sharding import PartitionSpec as P

MESH = pl.DeviceIdType.MESH
F32 = jnp.float32
BF16 = jnp.bfloat16


def kernel(
    side, bonds, segs,
    ids, counts, env, site, right,
    out, corr,
    e_all, a_all, w_acc, parts, right_in, term, terms_in,
    ring_send, ring_recv, e_send, e_recv, a_send, a_recv,
    right_send, right_recv, term_send, term_recv, local_sem, line_ready,
):
    chips = bonds // 2
    out_acc = out.at[0, 0]
    size = out_acc.shape[0]
    rows = size // 2
    seg = lax.axis_index("seg")
    bond = lax.axis_index("bond")
    z = bond // 2
    core = bond % 2
    row = bond // side
    column = bond % side
    half = z % 2
    turn = 1 - 2 * core

    def chip_at(step):
        return (z - turn * step + 2 * chips) % chips

    def mirrored(step):
        return (z + turn * step + 2 * chips) % chips

    def turned(chip):
        return (chip == chips // 4) | (chip == chips - 1 - chips // 4)

    def crossed(chip):
        return jnp.where(turned(chip) & (chip != z), 1, 0)

    def steps_from(chip, own_core):
        towards = jnp.where(own_core, z - chip, chip - z)
        return (towards * turn + 2 * chips) % chips

    following = (seg, ((z + turn + chips) % chips) * 2 + core)
    backward = (z - turn + chips) % chips
    sibling = (seg, z * 2 + 1 - core)
    has_before = seg > 0
    has_after = seg < segs - 1

    barrier = pltpu.get_barrier_semaphore()
    for peer in range(2):
        pl.semaphore_signal(barrier, inc=1, device_id=(seg, backward * 2 + peer), device_id_type=MESH)
    pl.semaphore_signal(barrier, inc=1, device_id=sibling, device_id_type=MESH)

    @pl.when(has_after)
    def _():
        pl.semaphore_signal(barrier, inc=1, device_id=(seg + 1, bond), device_id_type=MESH)

    own_env = pltpu.make_async_copy(env.at[0, 0], e_all.at[bond], local_sem.at[0])
    own_site = pltpu.make_async_copy(site.at[0, 0], a_all.at[z], local_sem.at[1])
    own_env.start()
    own_site.start()
    pl.semaphore_wait(barrier, 3 + jnp.where(has_before, 1, 0))

    def site_following(step):
        other = jnp.where(turned(z), step, 1) == 0
        return (seg, jnp.where(other, backward * 2 + 1 - core, following[1]))

    def ring_ref(step, part):
        chip = chip_at(step)
        if isinstance(part, int) and part >= 2:
            return a_all.at[chip, part - 2]
        return e_all.at[chip * 2 + core, pl.ds(part * rows, rows)]

    def ring_copy(step, part):
        ref = ring_ref(step, part)
        site_part = isinstance(part, int) and part >= 2
        return pltpu.make_async_remote_copy(
            src_ref=ref, dst_ref=ref,
            send_sem=ring_send.at[step * 4 + part], recv_sem=ring_recv.at[step * 4 + part],
            device_id=site_following(step) if site_part else following, device_id_type=MESH,
        )

    def ring_arrival(step, part):
        ref = ring_ref(step, part)
        return pltpu.make_async_remote_copy(
            src_ref=ref, dst_ref=ref,
            send_sem=ring_send.at[step * 4 - 4 + part], recv_sem=ring_recv.at[step * 4 - 4 + part],
            device_id=following, device_id_type=MESH,
        )

    def env_across(step, part, chip, at_core):
        ref = e_all.at[chip * 2 + at_core, pl.ds(part * rows, rows)]
        return pltpu.make_async_remote_copy(
            src_ref=ref, dst_ref=ref, send_sem=e_send.at[step * 2 + part], recv_sem=e_recv.at[step * 2 + part],
            device_id=sibling, device_id_type=MESH,
        )

    def site_across(chip, from_core, state):
        across_slot = jnp.where(column_of(chip, from_core) == row, chip // 2, side)
        return pltpu.make_async_remote_copy(
            src_ref=a_all.at[chip, state], dst_ref=a_all.at[chips + across_slot, state],
            send_sem=a_send.at[2 * across_slot + state], recv_sem=a_recv.at[2 * across_slot + state],
            device_id=sibling, device_id_type=MESH,
        )

    def column_of(chip, at_core):
        return 2 * (chip % 2) + (at_core + crossed(chip)) % 2

    def needed_across(chip, from_core):
        found = column_of(chip, from_core)
        return (found == row) | (found == 2 * half + 1 - from_core)

    own_site.wait()
    ring_copy(0, 2).start()
    ring_copy(0, 3).start()
    own_env.wait()
    ring_copy(0, 0).start()
    ring_copy(0, 1).start()
    env_across(0, 0, z, core).start()
    env_across(0, 1, z, core).start()

    @pl.when(needed_across(z, core))
    def _():
        for state in range(2):
            site_across(z, core, state).start()

    @pl.when(has_before)
    def _():
        pltpu.make_async_remote_copy(
            src_ref=right.at[0, 0], dst_ref=right_in, send_sem=right_send, recv_sem=right_recv,
            device_id=(seg - 1, bond), device_id_type=MESH,
        ).start()

    w_acc[...] = jnp.zeros_like(w_acc)
    out_acc[...] = jnp.zeros_like(out_acc)

    tally = [jnp.float32(0.0)] * 3
    for k in range(ids.shape[1]):
        for c in range(3):
            tally[c] = tally[c] + jnp.where((k < counts[0]) & (ids[0, k] == c), jnp.float32(1.0), jnp.float32(0.0))
    doubled = ((tally[0], tally[1] + tally[2]), (tally[1] - tally[2], -tally[0]))

    def env_phase(a, k):
        mine = k % 2 == core
        return 6 * steps_from(2 * a + k // 2, mine) + jnp.where(mine, 2, 4)

    def site_phase(chip, at_core):
        mine = at_core == core
        return 6 * steps_from(chip, mine) + jnp.where(mine, 0, 1)

    def column_phase(k):
        chip = 2 * k + half
        return site_phase(chip, (core + crossed(chip)) % 2)

    def column_slot(k):
        chip = 2 * k + half
        return jnp.where(crossed(chip) == 0, chip, chips + jnp.where(column == row, k, side))

    def left_phase(a):
        chip = 2 * a + row // 2
        return site_phase(chip, (row + crossed(chip)) % 2)

    def left_slot(a):
        chip = 2 * a + row // 2
        return jnp.where((row + crossed(chip)) % 2 == core, chip, chips + a)

    all_columns = jnp.int32(0)
    for k in range(side):
        all_columns = jnp.maximum(all_columns, column_phase(k))
    last_env = []
    last_site = []
    for a in range(side):
        latest = env_phase(a, 0)
        for k in range(1, side):
            latest = jnp.maximum(latest, env_phase(a, k))
        last_env.append(latest)
        last_site.append(jnp.maximum(all_columns, left_phase(a)))

    def picked(values, a):
        found = values[side - 1]
        for at in range(side - 1):
            found = jnp.where(a == at, values[at], found)
        return found

    def add_product(a, k, part, states):
        block = e_all[a * side + k, pl.ds(part * rows, rows)]
        slot = column_slot(k)
        for t in states:
            w_acc[a, t, pl.ds(part * rows, rows)] += jnp.dot(block, a_all[slot, t], preferred_element_type=F32)

    def finish(a, part, phase):
        @pl.when(jnp.maximum(picked(last_env, a) + part, picked(last_site, a)) == phase)
        def _():
            here = pl.ds(part * rows, rows)
            for s in range(2):
                weighted = doubled[s][0] * w_acc[a, 0, here] + doubled[s][1] * w_acc[a, 1, here]
                high = weighted.astype(BF16)
                parts[s * rows : (s + 1) * rows] = high
                parts[size + s * rows : size + (s + 1) * rows] = (weighted - high.astype(F32)).astype(BF16)
            left = a_all[left_slot(a), :, here].reshape(size, size)
            twice = jnp.concatenate([left, left], axis=0)
            out_acc[...] += lax.dot_general(twice, parts[...], (((0,), (0,)), ((), ())), preferred_element_type=F32)

    def take_env(chip, at_core, part, phase):
        a = chip // 2
        k = 2 * (chip % 2) + at_core

        @pl.when(column_phase(k) < phase)
        def _():
            add_product(a, k, part, (0, 1))

        finish(a, part, phase)

    def take_site(chip, at_core, phase, state):
        k = chip // 2

        def one(i, carry):
            a = i // 2
            part = i % 2

            @pl.when(env_phase(a, k) + part < phase)
            def _():
                add_product(a, k, part, (state,))

            return carry

        @pl.when(column_of(chip, at_core) == column)
        def _():
            lax.fori_loop(0, 2 * side, one, 0)

    def finish_site(chip, at_core, phase):
        found = column_of(chip, at_core)

        def one(i, carry):
            finish(i // 2, i % 2, phase)
            return carry

        @pl.when((found == column) | (found == row))
        def _():
            lax.fori_loop(0, 2 * side, one, 0)

    def env_comes(step, part):
        @pl.when(step > 0)
        def _():
            ring_arrival(step, part).wait_recv()
            ring_copy(step, part).start()
            env_across(step, part, chip_at(step), core).start()

    def own_halves(step):
        def one(part, carry):
            take_env(chip_at(step), core, part, 6 * step + 2 + part)
            return carry

        lax.fori_loop(0, 2, one, 0)

    def across_halves(step):
        chip = mirrored(step)

        def one(part, carry):
            env_across(step, part, chip, 1 - core).wait_recv()
            take_env(chip, 1 - core, part, 6 * step + 4 + part)
            return carry

        lax.fori_loop(0, 2, one, 0)

    def own_site(step, state):
        chip = chip_at(step)

        @pl.when(step > 0)
        def _():
            ring_arrival(step, 2 + state).wait_recv()

            @pl.when(step < chips - 2)
            def _():
                ring_copy(step, 2 + state).start()

            @pl.when(needed_across(chip, core))
            def _():
                site_across(chip, core, state).start()

        take_site(chip, core, 6 * step, state)

    def sibling_site(step, state):
        chip = mirrored(step)

        @pl.when(column_of(chip, 1 - core) == column)
        def _():
            site_across(chip, 1 - core, state).wait_recv()
            take_site(chip, 1 - core, 6 * step + 1, state)

    def turn_of(step, carry):
        own_site(step, 0)
        sibling_site(step, 0)
        own_site(step, 1)
        env_comes(step, 0)
        sibling_site(step, 1)
        env_comes(step, 1)
        own_halves(step)
        finish_site(chip_at(step), core, 6 * step)
        chip = mirrored(step)

        @pl.when(needed_across(chip, 1 - core))
        def _():
            @pl.when(column_of(chip, 1 - core) != column)
            def _():
                for state in range(2):
                    site_across(chip, 1 - core, state).wait_recv()

            finish_site(chip, 1 - core, 6 * step + 1)

        @pl.when((step == chips // 2 + 1) & has_before)
        def _():
            pl.semaphore_signal(line_ready, inc=1, device_id=(seg - 1, bond), device_id_type=MESH)

        across_halves(step)
        return carry

    lax.fori_loop(0, chips - 1, turn_of, 0)

    def last_turn(part, carry):
        step = chips - 1
        ring_arrival(step, part).wait_recv()
        env_across(step, part, chip_at(step), core).start()
        take_env(chip_at(step), core, part, 6 * step + 2 + part)
        env_across(step, part, mirrored(step), 1 - core).wait_recv()
        take_env(mirrored(step), 1 - core, part, 6 * step + 4 + part)
        return carry

    lax.fori_loop(0, 2, last_turn, 0)

    @pl.when(has_after)
    def _():
        pltpu.make_async_remote_copy(
            src_ref=right.at[0, 0], dst_ref=right_in, send_sem=right_send, recv_sem=right_recv,
            device_id=(seg, bond), device_id_type=MESH,
        ).wait_recv()
        products = out_acc[...] * right_in[...].astype(F32)
        folded = jnp.sum(products.reshape(size // 8, 8, size), axis=0)
        total = folded[:, :128]
        for at in range(128, size, 128):
            total = total + folded[:, at : at + 128]
        term[...] = total
        pl.semaphore_wait(line_ready, 1)
        for peer in range(bonds):
            pltpu.make_async_remote_copy(
                src_ref=term, dst_ref=terms_in.at[bond], send_sem=term_send.at[peer], recv_sem=term_recv,
                device_id=(seg + 1, peer), device_id_type=MESH,
            ).start()

    corr[0] = jnp.float32(0.0)

    @pl.when(has_before)
    def _():
        pltpu.make_async_remote_copy(
            src_ref=terms_in, dst_ref=terms_in, send_sem=term_send.at[0], recv_sem=term_recv,
            device_id=(seg, bond), device_id_type=MESH,
        ).wait_recv()
        corr[0] = jnp.sum(terms_in[...]) * (0.5 / (size * side))
        pltpu.make_async_remote_copy(
            src_ref=right.at[0, 0], dst_ref=right_in, send_sem=right_send, recv_sem=right_recv,
            device_id=(seg, bond), device_id_type=MESH,
        ).wait_send()

    @pl.when(has_after)
    def _():
        for peer in range(bonds):
            pltpu.make_async_remote_copy(
                src_ref=term, dst_ref=terms_in.at[bond], send_sem=term_send.at[peer], recv_sem=term_recv,
                device_id=(seg, bond), device_id_type=MESH,
            ).wait_send()

    def drain(step, carry):
        @pl.when(step < chips - 1)
        def _():
            ring_copy(step, 0).wait_send()
            ring_copy(step, 1).wait_send()

        @pl.when(step < chips - 2)
        def _():
            ring_copy(step, 2).wait_send()
            ring_copy(step, 3).wait_send()

        env_across(step, 0, chip_at(step), core).wait_send()
        env_across(step, 1, chip_at(step), core).wait_send()

        @pl.when((step < chips - 1) & needed_across(chip_at(step), core))
        def _():
            for state in range(2):
                site_across(chip_at(step), core, state).wait_send()

        return carry

    lax.fori_loop(0, chips, drain, 0)


def body(env_in, site, right_env, comp_ids, counts):
    bonds = lax.axis_size("bond")
    segs = lax.axis_size("seg")
    side = math.isqrt(bonds)
    chips = bonds // 2
    size = env_in.shape[-1]
    hbm = pl.BlockSpec(memory_space=pltpu.HBM)
    smem = pl.BlockSpec(memory_space=pltpu.SMEM)
    dma = pltpu.SemaphoreType.DMA
    twice, closed = pl.pallas_call(
        functools.partial(kernel, side, bonds, segs),
        out_shape=(
            pltpu.VMEM((1, 1, size, size), F32),
            jax.ShapeDtypeStruct((1,), F32),
        ),
        in_specs=[smem, smem, hbm, hbm, hbm],
        out_specs=(pl.BlockSpec(memory_space=pltpu.VMEM), smem),
        scratch_shapes=[
            pltpu.VMEM((bonds, size, size), BF16),
            pltpu.VMEM((chips + side + 1, 2, size, size), BF16),
            pltpu.VMEM((side, 2, size, size), F32),
            pltpu.VMEM((2 * size, size), BF16),
            pltpu.VMEM((size, size), BF16),
            pltpu.VMEM((8, 128), F32),
            pltpu.VMEM((bonds, 8, 128), F32),
            dma((4 * (chips - 1),)),
            dma((4 * (chips - 1),)),
            dma((2 * chips,)),
            dma((2 * chips,)),
            dma((2 * side + 2,)),
            dma((2 * side + 2,)),
            dma,
            dma,
            dma((bonds,)),
            dma,
            dma((2,)),
            pltpu.SemaphoreType.REGULAR,
        ],
        compiler_params=pltpu.CompilerParams(
            collective_id=0, has_side_effects=True, vmem_limit_bytes=56 * 2**20
        ),
        cost_estimate=pl.CostEstimate(flops=26 * 10**9, bytes_accessed=6 * 2**20, transcendentals=0),
    )(comp_ids, counts, env_in, site, right_env)
    return twice * 0.5, closed


def solution(mesh):
    placed = (
        P("seg", "bond", None, None),
        P("seg", "bond", None, None, None),
        P("seg", "bond", None, None),
        P("seg", None),
        P("seg"),
    )
    return jax.shard_map(
        body,
        mesh=mesh,
        in_specs=placed,
        out_specs=(P("seg", "bond", None, None), P("seg")),
        check_vma=False,
    )
```
